32 devices in a mesh: layer: 4 (over z), prow: 2 (over y), pcol: 4 (over x, core).
Axes of the slice: x: 2, y: 2, z: 4, core: 2. Of those that a mesh axis runs over, the one named last changes fastest.
Arguments:
- front: bfloat16 [3072, 3072], P('prow', 'pcol')
- lower_desc: bfloat16 [3072, 2048], P('prow', 'layer')
- upper_desc: bfloat16 [2048, 3072], P('layer', 'pcol')
- pattern: int32 [4, 32], P('layer'), may hold values 0 or 1
- pivot: int32 [16, 192], P('prow'), may hold values from 0 to 191, as said below
Outputs:
- factored: float32 [3072, 3072], P('prow', 'pcol')
The draws below stay inside these ranges and needn't reach their ends.
Inputs may be any that keep to these rules, and one draw needn't show every extreme that they name: Each row of pivot lists every offset 0 to 191 once.
All inputs are finite; a program needn't handle non-finite values. No bound on the sum of `pattern` on one device may be relied on, other than what follows from the above.
Results may differ from the reference program's by a relative error of at most 0.0003.
Values sent between devices are 32-bit elements; how exact they have to be, the bound alone decides.
A program may use at most 64 MiB of HBM per device.

```python
import math
import jax
import jax.numpy as jnp
from jax import lax

BLOCK = 192
PW = 3072
WD = 512
KSTEP = 4
NR = 3072
LAYERS = 4
GRID_ROWS = 2
GRID_COLS = 4


def pivot_table(key):
    keys = jax.random.split(jax.random.fold_in(key, 11), NR // BLOCK)

    def shuffle(single):
        return jax.random.permutation(single, BLOCK)
    return jax.vmap(shuffle)(keys).astype(jnp.int32)


def logical_positions(length, groups):
    place = jnp.arange(length, dtype=jnp.int32)
    per_group = length // BLOCK // groups
    blocks = place // BLOCK
    return (blocks % per_group * groups + blocks // per_group) * BLOCK + place % BLOCK


def draw_pivot(key, part):
    return pivot_table(key)


def draw_front(key, part):
    pivot = pivot_table(key)
    noise_key = jax.random.fold_in(key, 29)
    diag_key = jax.random.fold_in(key, 31)
    noise = jnp.clip(jax.random.normal(noise_key, (NR, PW), jnp.float32), -4.0, 4.0)
    low_weight = math.log(56.0)
    high_weight = math.log(448.0)
    weights = jnp.exp(jax.random.uniform(diag_key, (NR,), jnp.float32, low_weight, high_weight))
    logical_rows = logical_positions(NR, GRID_ROWS)
    target_cols = logical_rows // BLOCK * BLOCK + (logical_rows % BLOCK + 1) % BLOCK
    matches = target_cols[:, None] == logical_positions(PW, GRID_COLS)[None, :]
    hits = matches.astype(jnp.float32) * weights[:, None]
    source = (jnp.arange(NR // BLOCK, dtype=jnp.int32)[:, None] * BLOCK + pivot).reshape(-1)
    placed = jnp.zeros((NR, PW), jnp.float32).at[source].add(hits)
    return (noise + placed).astype(jnp.bfloat16)


def scaled_draw(key, shape, spread):
    values = jnp.clip(jax.random.normal(key, shape, jnp.float32), -4.0, 4.0)
    return (values * spread).astype(jnp.bfloat16)


def draw_lower_desc(key, part):
    return scaled_draw(jax.random.fold_in(key, 41), (NR, WD * LAYERS), WD ** (-0.5))


def draw_upper_desc(key, part):
    return scaled_draw(jax.random.fold_in(key, 43), (WD * LAYERS, PW), 0.25)


def touch_ends(entries, own_key, smallest, top_value):
    spot = [jax.random.randint(jax.random.fold_in(own_key, axis), (), 0, length) for axis, length in enumerate(entries.shape)]
    widest = entries.shape.index(max(entries.shape))
    beside = spot[:widest] + [(spot[widest] + 1) % entries.shape[widest]] + spot[widest + 1:]
    return entries.at[tuple(spot)].set(smallest).at[tuple(beside)].set(top_value)


def setup_inputs(seed: int = 0) -> dict:
    arg_keys = jax.random.split(jax.random.key(seed), 6)
    front = draw_front(jax.random.fold_in(arg_keys[5], 71), 0)
    lower_desc = draw_lower_desc(jax.random.fold_in(arg_keys[5], 71), 0)
    upper_desc = draw_upper_desc(jax.random.fold_in(arg_keys[5], 71), 0)
    pattern = touch_ends((jax.random.randint(arg_keys[3], (LAYERS, NR // BLOCK + PW // BLOCK), 0, 4) < 3).astype(jnp.int32), jax.random.fold_in(arg_keys[3], 1), 0, 1)
    pivot = draw_pivot(jax.random.fold_in(arg_keys[5], 71), 0)
    return dict(front=front, lower_desc=lower_desc, upper_desc=upper_desc, pattern=pattern, pivot=pivot)


PRECISE = lax.Precision.HIGHEST

def to_logical(matrix, groups, axis):
    count_blocks = matrix.shape[axis] // BLOCK
    shaped = matrix.reshape(matrix.shape[:axis] + (groups, count_blocks // groups, BLOCK) + matrix.shape[axis + 1:])
    return jnp.swapaxes(shaped, axis, axis + 1).reshape(matrix.shape)

def to_stored(matrix, groups, axis):
    count_blocks = matrix.shape[axis] // BLOCK
    shaped = matrix.reshape(matrix.shape[:axis] + (count_blocks // groups, groups, BLOCK) + matrix.shape[axis + 1:])
    return jnp.swapaxes(shaped, axis, axis + 1).reshape(matrix.shape)

def reference(front, lower_desc, upper_desc, pattern, pivot):
    row_blocks = NR // BLOCK

    def add_layer(total, layer):
        lower_part = lax.dynamic_slice_in_dim(lower_desc, layer * WD, WD, 1)
        upper_part = lax.dynamic_slice_in_dim(upper_desc, layer * WD, WD, 0)
        layer_flags = pattern[layer]
        row_keep = jnp.repeat(layer_flags[:row_blocks], BLOCK).astype(lower_desc.dtype)
        col_keep = jnp.repeat(layer_flags[row_blocks:], BLOCK).astype(upper_desc.dtype)
        product = jnp.dot((lower_part * row_keep[:, None]).astype(jnp.float32), (upper_part * col_keep[None, :]).astype(jnp.float32), preferred_element_type=jnp.float32)
        return (total + product, None)
    update, _ = lax.scan(add_layer, jnp.zeros((NR, PW), jnp.float32), jnp.arange(LAYERS, dtype=jnp.int32))
    assembled = front.astype(jnp.float32) - update
    source = (jnp.arange(row_blocks, dtype=jnp.int32)[:, None] * BLOCK + pivot).reshape(-1)
    pivoted = to_logical(to_logical(assembled[source], GRID_ROWS, 0), GRID_COLS, 1)
    for section in range(KSTEP):
        first_row = section * BLOCK
        past_row = first_row + BLOCK
        inverse = jnp.linalg.inv(pivoted[first_row:past_row, first_row:past_row])
        multipliers = jnp.dot(pivoted[past_row:, first_row:past_row], inverse, precision=PRECISE)
        trailing = pivoted[past_row:, past_row:] - jnp.dot(multipliers, pivoted[first_row:past_row, past_row:], precision=PRECISE)
        pivoted = pivoted.at[past_row:, past_row:].set(trailing)
        pivoted = pivoted.at[past_row:, first_row:past_row].set(multipliers)
    return to_stored(to_stored(pivoted, GRID_ROWS, 0), GRID_COLS, 1)
```

```python
import functools

import jax
import jax.numpy as jnp
from jax import lax
from jax.experimental import pallas as pl
from jax.experimental.pallas import tpu as pltpu
from jax.sharding import PartitionSpec as P

KSTEP = 4
FINE = lax.Precision.HIGHEST
HIGH = lax.Precision.HIGH


def coarse_dot(a, b):
    return jnp.dot(a.astype(jnp.bfloat16), b.astype(jnp.bfloat16), preferred_element_type=jnp.float32)


def fine_dot(a, b):
    return jnp.dot(a, b, precision=FINE, preferred_element_type=jnp.float32)


def gram_bound(scaled):
    low = scaled.astype(jnp.bfloat16)
    gram = lax.dot_general(low, low, (((1,), (1,)), ((), ())), preferred_element_type=jnp.float32)
    return 0.98 / jnp.max(jnp.sum(jnp.abs(gram), axis=1, keepdims=True))


def factor_kernel(a_ref, f_ref, inv_ref, x_ref, r_ref, s_ref):
    size = a_ref.shape[2]
    row = lax.broadcasted_iota(jnp.int32, (size, size), 0)
    col = lax.broadcasted_iota(jnp.int32, (size, size), 1)
    eye = jnp.where(row == col, 1.0, 0.0).astype(jnp.float32)
    f_ref[...] = a_ref[...]

    for b in range(KSTEP):
        block = a_ref[b, b]
        peak = jnp.max(jnp.abs(block), axis=1, keepdims=True)
        scale = jnp.where(peak > 0.0, 1.0 / jnp.where(peak > 0.0, peak, 1.0), 1.0)
        s_ref[b] = jnp.broadcast_to(scale, (size, size))
        scaled = block * scale
        start = scaled.T * gram_bound(scaled)
        x_ref[b] = start
        r_ref[b] = eye - coarse_dot(scaled, start)

    def worst():
        return functools.reduce(jnp.maximum, [jnp.sum(r_ref[b] * r_ref[b]) for b in range(KSTEP)])

    def coarse(state):
        for b in range(KSTEP):
            left = r_ref[b]
            start = x_ref[b]
            once = start + coarse_dot(start, left)
            twice = once + coarse_dot(once, coarse_dot(left, left))
            x_ref[b] = twice
            r_ref[b] = eye - coarse_dot(a_ref[b, b] * s_ref[b], twice)
        return state[0] + 1, worst()

    lax.while_loop(lambda s: (s[1] > 0.1) & (s[0] < 12), coarse, (jnp.int32(0), worst()))

    for k in range(KSTEP):
        scale = s_ref[k]
        scaled = f_ref[k, k] * scale
        r_ref[k] = eye - fine_dot(scaled, x_ref[k])
        near = jnp.sum(r_ref[k] * r_ref[k])

        @pl.when(jnp.logical_not(near < 0.5))
        def restart():
            start = scaled.T * gram_bound(scaled)
            x_ref[k] = start
            r_ref[k] = eye - fine_dot(scaled, start)

        def fine(state):
            x_ref[k] = x_ref[k] + fine_dot(x_ref[k], r_ref[k])
            left = eye - fine_dot(f_ref[k, k] * s_ref[k], x_ref[k])
            r_ref[k] = left
            return state[0] + 1, jnp.sum(left * left)

        lax.while_loop(
            lambda s: (s[1] > 1e-6) & (s[0] < 60), fine, (jnp.int32(0), jnp.sum(r_ref[k] * r_ref[k]))
        )
        across = jnp.sum(eye * scale, axis=0, keepdims=True)
        inverse = (x_ref[k] + fine_dot(x_ref[k], r_ref[k])) * across
        inv_ref[k] = inverse
        for i in range(k + 1, KSTEP):
            f_ref[i, k] = fine_dot(f_ref[i, k], inverse)
            for j in range(k + 1, KSTEP):
                f_ref[i, j] = f_ref[i, j] - fine_dot(f_ref[i, k], f_ref[k, j])


def factor(blocks):
    size = blocks.shape[2]
    return pl.pallas_call(
        factor_kernel,
        out_shape=(
            jax.ShapeDtypeStruct(blocks.shape, jnp.float32),
            jax.ShapeDtypeStruct((KSTEP, size, size), jnp.float32),
        ),
        in_specs=[pl.BlockSpec(memory_space=pltpu.VMEM)],
        out_specs=(pl.BlockSpec(memory_space=pltpu.VMEM), pl.BlockSpec(memory_space=pltpu.VMEM)),
        scratch_shapes=[pltpu.VMEM((KSTEP, size, size), jnp.float32)] * 3,
        compiler_params=pltpu.CompilerParams(vmem_limit_bytes=40 * 1024 * 1024),
        cost_estimate=pl.CostEstimate(flops=40_000_000_000, bytes_accessed=8_000_000, transcendentals=0),
        name="factor",
    )(blocks)


def shards(front, lower_desc, upper_desc, pattern, pivot):
    rows_dev, cols_dev = front.shape
    row_blocks, size = pivot.shape
    grid_rows = lax.axis_size("prow")
    grid_cols = lax.axis_size("pcol")
    own_row = lax.axis_index("prow")
    own_col = lax.axis_index("pcol")
    col_blocks = cols_dev // size
    top_rows = -(-KSTEP // grid_rows) * size
    top_cols = -(-KSTEP // grid_cols) * size
    flags = pattern[0].astype(jnp.bfloat16)
    row_flags = lax.dynamic_slice_in_dim(flags, own_row * row_blocks, row_blocks)
    col_flags = lax.dynamic_slice_in_dim(flags, row_blocks * grid_rows + own_col * col_blocks, col_blocks)
    onehot = (pivot[:, :, None] == jnp.arange(size, dtype=jnp.int32)).astype(jnp.bfloat16)

    def permute(values, weights, kind):
        blocked = values.reshape(row_blocks, size, values.shape[1])
        return jnp.einsum("bij,bjn->bin", weights, blocked, preferred_element_type=kind).reshape(values.shape)

    lower = permute(lower_desc, onehot * row_flags[:, None, None], jnp.bfloat16)
    upper = upper_desc * jnp.repeat(col_flags, size)[None, :]
    initial = permute(front, onehot, jnp.float32)

    def assembled(rows, cols):
        part = jnp.dot(lower[rows], upper[:, cols], preferred_element_type=jnp.float32)
        return initial[rows, cols] - lax.psum(part, "layer")

    left, right = slice(0, top_cols), slice(top_cols, None)
    top, below = slice(0, top_rows), slice(top_rows, None)
    own_left = assembled(slice(0, None), left)
    own_top = jnp.concatenate([own_left[top], assembled(top, right)], axis=1)
    rest = assembled(below, right)

    corner = lax.all_gather(lax.all_gather(own_left[top], "pcol"), "prow")

    def block(array, r, c):
        return array[r * size : (r + 1) * size, c * size : (c + 1) * size]

    leading = jnp.stack([
        jnp.stack([
            block(corner[i % grid_rows, j % grid_cols], i // grid_rows, j // grid_cols)
            for j in range(KSTEP)
        ])
        for i in range(KSTEP)
    ])
    columns = lax.all_gather(own_left[below], "pcol")
    tops = lax.all_gather(own_top, "prow")
    packed, inverses = factor(leading)

    upper_rows = []
    for k in range(KSTEP):
        start = k // grid_rows * size
        value = tops[k % grid_rows, start : start + size]
        for j in range(k):
            value = value - jnp.dot(packed[k, j], upper_rows[j], precision=HIGH)
        upper_rows.append(value)
    lower_cols = []
    for k in range(KSTEP):
        start = k // grid_cols * size
        value = columns[k % grid_cols, :, start : start + size]
        for j in range(k):
            value = value - jnp.dot(lower_cols[j], packed[j, k], precision=HIGH)
        lower_cols.append(jnp.dot(value, inverses[k], precision=FINE))
    upper_all = jnp.concatenate(upper_rows, axis=0)
    lower_all = jnp.concatenate(lower_cols, axis=1)

    def trailing(values, multipliers, cols):
        return values - jnp.dot(multipliers, upper_all[:, cols], precision=HIGH)

    def pick(choices, index):
        return lax.dynamic_index_in_dim(choices, index, 0, keepdims=False)

    own_below = jnp.concatenate(
        [
            jnp.where(
                t * grid_cols + own_col < KSTEP,
                pick(jnp.stack(lower_cols), jnp.minimum(t * grid_cols + own_col, KSTEP - 1)),
                trailing(own_left[below, t * size : (t + 1) * size], lower_all, slice(t * size, (t + 1) * size)),
            )
            if grid_cols * (t + 1) > KSTEP
            else pick(jnp.stack(lower_cols), t * grid_cols + own_col)
            for t in range(top_cols // size)
        ]
        + [trailing(rest, lower_all, right)],
        axis=1,
    )
    tops_out = []
    row_stack = jnp.stack(upper_rows)
    for t in range(top_rows // size):
        logical = t * grid_rows + own_row
        if grid_rows * (t + 1) <= KSTEP:
            index = logical
        else:
            index = jnp.minimum(logical, KSTEP - 1)
        value = pick(row_stack, index)
        factors = pick(packed, index)
        pieces = []
        for c in range(top_cols // size):
            column = c * grid_cols + own_col
            inner = pick(factors, jnp.minimum(column, KSTEP - 1))
            pieces.append(jnp.where(column < KSTEP, inner, value[:, c * size : (c + 1) * size]))
        value = jnp.concatenate(pieces + [value[:, top_cols:]], axis=1)
        if grid_rows * (t + 1) > KSTEP:
            source = own_top[t * size : (t + 1) * size]
            lows = []
            own_columns = lax.all_gather(source[:, :top_cols], "pcol")
            for k in range(KSTEP):
                start = k // grid_cols * size
                part = own_columns[k % grid_cols, :, start : start + size]
                for j in range(k):
                    part = part - jnp.dot(lows[j], packed[j, k], precision=HIGH)
                lows.append(jnp.dot(part, inverses[k], precision=FINE))
            full = source - jnp.dot(jnp.concatenate(lows, axis=1), upper_all, precision=HIGH)
            pieces = []
            for c in range(top_cols // size):
                column = c * grid_cols + own_col
                inner = pick(jnp.stack(lows), jnp.minimum(column, KSTEP - 1))
                pieces.append(jnp.where(column < KSTEP, inner, full[:, c * size : (c + 1) * size]))
            full = jnp.concatenate(pieces + [full[:, top_cols:]], axis=1)
            value = jnp.where(logical < KSTEP, value, full)
        tops_out.append(value)
    return jnp.concatenate(tops_out + [own_below], axis=0)


def solution(mesh):
    return jax.shard_map(
        shards,
        mesh=mesh,
        in_specs=(
            P("prow", "pcol"),
            P("prow", "layer"),
            P("layer", "pcol"),
            P("layer", None),
            P("prow", None),
        ),
        out_specs=P("prow", "pcol"),
        check_vma=False,
    )
```

```python
import functools

import jax
import jax.numpy as jnp
from jax import lax
from jax.experimental import pallas as pl
from jax.experimental.pallas import tpu as pltpu
from jax.sharding import PartitionSpec as P

KSTEP = 4
FINE = lax.Precision.HIGHEST
HIGH = lax.Precision.HIGH


def coarse_dot(a, b):
    return jnp.dot(a.astype(jnp.bfloat16), b.astype(jnp.bfloat16), preferred_element_type=jnp.float32)


def fine_dot(a, b):
    return jnp.dot(a, b, precision=FINE, preferred_element_type=jnp.float32)


def gram_bound(scaled):
    low = scaled.astype(jnp.bfloat16)
    gram = lax.dot_general(low, low, (((1,), (1,)), ((), ())), preferred_element_type=jnp.float32)
    return 0.98 / jnp.max(jnp.sum(jnp.abs(gram), axis=1, keepdims=True))


def factor_kernel(a_ref, f_ref, inv_ref, x_ref, r_ref, s_ref):
    size = a_ref.shape[2]
    row = lax.broadcasted_iota(jnp.int32, (size, size), 0)
    col = lax.broadcasted_iota(jnp.int32, (size, size), 1)
    eye = jnp.where(row == col, 1.0, 0.0).astype(jnp.float32)
    f_ref[...] = a_ref[...]

    for b in range(KSTEP):
        block = a_ref[b, b]
        peak = jnp.max(jnp.abs(block), axis=1, keepdims=True)
        scale = jnp.where(peak > 0.0, 1.0 / jnp.where(peak > 0.0, peak, 1.0), 1.0)
        s_ref[b] = jnp.broadcast_to(scale, (size, size))
        scaled = block * scale
        start = scaled.T * gram_bound(scaled)
        x_ref[b] = start
        r_ref[b] = eye - coarse_dot(scaled, start)

    def worst():
        return functools.reduce(jnp.maximum, [jnp.sum(r_ref[b] * r_ref[b]) for b in range(KSTEP)])

    def coarse(state):
        for b in range(KSTEP):
            left = r_ref[b]
            start = x_ref[b]
            once = start + coarse_dot(start, left)
            twice = once + coarse_dot(once, coarse_dot(left, left))
            x_ref[b] = twice
            r_ref[b] = eye - coarse_dot(a_ref[b, b] * s_ref[b], twice)
        return state[0] + 1, worst()

    lax.while_loop(lambda s: (s[1] > 0.1) & (s[0] < 12), coarse, (jnp.int32(0), worst()))

    for k in range(KSTEP):
        scale = s_ref[k]
        scaled = f_ref[k, k] * scale
        r_ref[k] = eye - fine_dot(scaled, x_ref[k])
        near = jnp.sum(r_ref[k] * r_ref[k])

        @pl.when(jnp.logical_not(near < 0.5))
        def restart():
            start = scaled.T * gram_bound(scaled)
            x_ref[k] = start
            r_ref[k] = eye - fine_dot(scaled, start)

        def fine(state):
            x_ref[k] = x_ref[k] + fine_dot(x_ref[k], r_ref[k])
            left = eye - fine_dot(f_ref[k, k] * s_ref[k], x_ref[k])
            r_ref[k] = left
            return state[0] + 1, jnp.sum(left * left)

        lax.while_loop(
            lambda s: (s[1] > 1e-6) & (s[0] < 60), fine, (jnp.int32(0), jnp.sum(r_ref[k] * r_ref[k]))
        )
        across = jnp.sum(eye * scale, axis=0, keepdims=True)
        inverse = (x_ref[k] + fine_dot(x_ref[k], r_ref[k])) * across
        inv_ref[k] = inverse
        for i in range(k + 1, KSTEP):
            f_ref[i, k] = fine_dot(f_ref[i, k], inverse)
            for j in range(k + 1, KSTEP):
                f_ref[i, j] = f_ref[i, j] - fine_dot(f_ref[i, k], f_ref[k, j])


def factor(blocks):
    size = blocks.shape[2]
    return pl.pallas_call(
        factor_kernel,
        out_shape=(
            jax.ShapeDtypeStruct(blocks.shape, jnp.float32),
            jax.ShapeDtypeStruct((KSTEP, size, size), jnp.float32),
        ),
        in_specs=[pl.BlockSpec(memory_space=pltpu.VMEM)],
        out_specs=(pl.BlockSpec(memory_space=pltpu.VMEM), pl.BlockSpec(memory_space=pltpu.VMEM)),
        scratch_shapes=[pltpu.VMEM((KSTEP, size, size), jnp.float32)] * 3,
        compiler_params=pltpu.CompilerParams(vmem_limit_bytes=40 * 1024 * 1024),
        cost_estimate=pl.CostEstimate(flops=40_000_000_000, bytes_accessed=8_000_000, transcendentals=0),
        name="factor",
    )(blocks)


def shards(front, lower_desc, upper_desc, pattern, pivot):
    rows_dev, cols_dev = front.shape
    row_blocks, size = pivot.shape
    grid_rows = lax.axis_size("prow")
    grid_cols = lax.axis_size("pcol")
    own_row = lax.axis_index("prow")
    own_col = lax.axis_index("pcol")
    col_blocks = cols_dev // size
    top_rows = -(-KSTEP // grid_rows) * size
    top_cols = -(-KSTEP // grid_cols) * size
    flags = pattern[0].astype(jnp.bfloat16)
    row_flags = lax.dynamic_slice_in_dim(flags, own_row * row_blocks, row_blocks)
    col_flags = lax.dynamic_slice_in_dim(flags, row_blocks * grid_rows + own_col * col_blocks, col_blocks)
    onehot = (pivot[:, :, None] == jnp.arange(size, dtype=jnp.int32)).astype(jnp.bfloat16)

    def permute(values, weights, kind):
        blocked = values.reshape(row_blocks, size, values.shape[1])
        return jnp.einsum("bij,bjn->bin", weights, blocked, preferred_element_type=kind).reshape(values.shape)

    lower = permute(lower_desc, onehot * row_flags[:, None, None], jnp.bfloat16)
    upper = upper_desc * jnp.repeat(col_flags, size)[None, :]
    initial = permute(front, onehot, jnp.float32)

    def partial(rows, cols):
        return jnp.dot(lower[rows], upper[:, cols], preferred_element_type=jnp.float32)

    def assembled(rows, cols):
        return initial[rows, cols] - lax.psum(partial(rows, cols), "layer")

    left, right = slice(0, top_cols), slice(top_cols, None)
    top, below = slice(0, top_rows), slice(top_rows, None)
    own_left = assembled(slice(0, None), left)
    own_top = jnp.concatenate([own_left[top], assembled(top, right)], axis=1)
    corner = lax.all_gather(lax.all_gather(own_left[top], "pcol"), "prow")
    rest_part, corner, own_top = lax.optimization_barrier((partial(below, right), corner, own_top))
    rest = initial[below, right] - lax.psum(rest_part, "layer")

    def block(array, r, c):
        return array[r * size : (r + 1) * size, c * size : (c + 1) * size]

    leading = jnp.stack([
        jnp.stack([
            block(corner[i % grid_rows, j % grid_cols], i // grid_rows, j // grid_cols)
            for j in range(KSTEP)
        ])
        for i in range(KSTEP)
    ])
    columns = lax.all_gather(own_left[below], "pcol")
    tops = lax.all_gather(own_top, "prow")
    packed, inverses = factor(leading)

    upper_rows = []
    for k in range(KSTEP):
        start = k // grid_rows * size
        value = tops[k % grid_rows, start : start + size]
        for j in range(k):
            value = value - jnp.dot(packed[k, j], upper_rows[j], precision=HIGH)
        upper_rows.append(value)
    lower_cols = []
    for k in range(KSTEP):
        start = k // grid_cols * size
        value = columns[k % grid_cols, :, start : start + size]
        for j in range(k):
            value = value - jnp.dot(lower_cols[j], packed[j, k], precision=HIGH)
        lower_cols.append(jnp.dot(value, inverses[k], precision=FINE))
    upper_all = jnp.concatenate(upper_rows, axis=0)
    lower_all = jnp.concatenate(lower_cols, axis=1)

    def trailing(values, multipliers, cols):
        return values - jnp.dot(multipliers, upper_all[:, cols], precision=HIGH)

    def pick(choices, index):
        return lax.dynamic_index_in_dim(choices, index, 0, keepdims=False)

    own_below = jnp.concatenate(
        [
            jnp.where(
                t * grid_cols + own_col < KSTEP,
                pick(jnp.stack(lower_cols), jnp.minimum(t * grid_cols + own_col, KSTEP - 1)),
                trailing(own_left[below, t * size : (t + 1) * size], lower_all, slice(t * size, (t + 1) * size)),
            )
            if grid_cols * (t + 1) > KSTEP
            else pick(jnp.stack(lower_cols), t * grid_cols + own_col)
            for t in range(top_cols // size)
        ]
        + [trailing(rest, lower_all, right)],
        axis=1,
    )
    tops_out = []
    row_stack = jnp.stack(upper_rows)
    for t in range(top_rows // size):
        logical = t * grid_rows + own_row
        if grid_rows * (t + 1) <= KSTEP:
            index = logical
        else:
            index = jnp.minimum(logical, KSTEP - 1)
        value = pick(row_stack, index)
        factors = pick(packed, index)
        pieces = []
        for c in range(top_cols // size):
            column = c * grid_cols + own_col
            inner = pick(factors, jnp.minimum(column, KSTEP - 1))
            pieces.append(jnp.where(column < KSTEP, inner, value[:, c * size : (c + 1) * size]))
        value = jnp.concatenate(pieces + [value[:, top_cols:]], axis=1)
        if grid_rows * (t + 1) > KSTEP:
            source = own_top[t * size : (t + 1) * size]
            lows = []
            own_columns = lax.all_gather(source[:, :top_cols], "pcol")
            for k in range(KSTEP):
                start = k // grid_cols * size
                part = own_columns[k % grid_cols, :, start : start + size]
                for j in range(k):
                    part = part - jnp.dot(lows[j], packed[j, k], precision=HIGH)
                lows.append(jnp.dot(part, inverses[k], precision=FINE))
            full = source - jnp.dot(jnp.concatenate(lows, axis=1), upper_all, precision=HIGH)
            pieces = []
            for c in range(top_cols // size):
                column = c * grid_cols + own_col
                inner = pick(jnp.stack(lows), jnp.minimum(column, KSTEP - 1))
                pieces.append(jnp.where(column < KSTEP, inner, full[:, c * size : (c + 1) * size]))
            full = jnp.concatenate(pieces + [full[:, top_cols:]], axis=1)
            value = jnp.where(logical < KSTEP, value, full)
        tops_out.append(value)
    return jnp.concatenate(tops_out + [own_below], axis=0)


def solution(mesh):
    return jax.shard_map(
        shards,
        mesh=mesh,
        in_specs=(
            P("prow", "pcol"),
            P("prow", "layer"),
            P("layer", "pcol"),
            P("layer", None),
            P("prow", None),
        ),
        out_specs=P("prow", "pcol"),
        check_vma=False,
    )
```

```python
import functools

import jax
import jax.numpy as jnp
from jax import lax
from jax.experimental import pallas as pl
from jax.experimental.pallas import tpu as pltpu
from jax.sharding import PartitionSpec as P

KSTEP = 4
FINE = lax.Precision.HIGHEST
HIGH = lax.Precision.HIGH


def coarse_dot(a, b):
    return jnp.dot(a.astype(jnp.bfloat16), b.astype(jnp.bfloat16), preferred_element_type=jnp.float32)


def fine_dot(a, b):
    return jnp.dot(a, b, precision=FINE, preferred_element_type=jnp.float32)


def gram_bound(scaled):
    low = scaled.astype(jnp.bfloat16)
    gram = lax.dot_general(low, low, (((1,), (1,)), ((), ())), preferred_element_type=jnp.float32)
    return 0.98 / jnp.max(jnp.sum(jnp.abs(gram), axis=1, keepdims=True))


def factor_kernel(a_ref, f_ref, inv_ref, x_ref, r_ref, s_ref):
    size = a_ref.shape[2]
    row = lax.broadcasted_iota(jnp.int32, (size, size), 0)
    col = lax.broadcasted_iota(jnp.int32, (size, size), 1)
    eye = jnp.where(row == col, 1.0, 0.0).astype(jnp.float32)
    f_ref[...] = a_ref[...]

    for b in range(KSTEP):
        block = a_ref[b, b]
        peak = jnp.max(jnp.abs(block), axis=1, keepdims=True)
        scale = jnp.where(peak > 0.0, 1.0 / jnp.where(peak > 0.0, peak, 1.0), 1.0)
        s_ref[b] = jnp.broadcast_to(scale, (size, size))
        scaled = block * scale
        start = scaled.T * gram_bound(scaled)
        x_ref[b] = start
        r_ref[b] = eye - coarse_dot(scaled, start)

    def worst():
        return functools.reduce(jnp.maximum, [jnp.sum(r_ref[b] * r_ref[b]) for b in range(KSTEP)])

    def coarse(state):
        for b in range(KSTEP):
            left = r_ref[b]
            start = x_ref[b]
            once = start + coarse_dot(start, left)
            twice = once + coarse_dot(once, coarse_dot(left, left))
            x_ref[b] = twice
            r_ref[b] = eye - coarse_dot(a_ref[b, b] * s_ref[b], twice)
        return state[0] + 1, worst()

    lax.while_loop(lambda s: (s[1] > 0.1) & (s[0] < 12), coarse, (jnp.int32(0), worst()))

    for k in range(KSTEP):
        scale = s_ref[k]
        scaled = f_ref[k, k] * scale
        r_ref[k] = eye - fine_dot(scaled, x_ref[k])
        near = jnp.sum(r_ref[k] * r_ref[k])

        @pl.when(jnp.logical_not(near < 0.5))
        def restart():
            start = scaled.T * gram_bound(scaled)
            x_ref[k] = start
            r_ref[k] = eye - fine_dot(scaled, start)

        def fine(state):
            x_ref[k] = x_ref[k] + fine_dot(x_ref[k], r_ref[k])
            left = eye - fine_dot(f_ref[k, k] * s_ref[k], x_ref[k])
            r_ref[k] = left
            return state[0] + 1, jnp.sum(left * left)

        lax.while_loop(
            lambda s: (s[1] > 1e-6) & (s[0] < 60), fine, (jnp.int32(0), jnp.sum(r_ref[k] * r_ref[k]))
        )
        across = jnp.sum(eye * scale, axis=0, keepdims=True)
        inverse = (x_ref[k] + fine_dot(x_ref[k], r_ref[k])) * across
        inv_ref[k] = inverse
        for i in range(k + 1, KSTEP):
            f_ref[i, k] = fine_dot(f_ref[i, k], inverse)
            for j in range(k + 1, KSTEP):
                f_ref[i, j] = f_ref[i, j] - fine_dot(f_ref[i, k], f_ref[k, j])


def factor(blocks):
    size = blocks.shape[2]
    return pl.pallas_call(
        factor_kernel,
        out_shape=(
            jax.ShapeDtypeStruct(blocks.shape, jnp.float32),
            jax.ShapeDtypeStruct((KSTEP, size, size), jnp.float32),
        ),
        in_specs=[pl.BlockSpec(memory_space=pltpu.VMEM)],
        out_specs=(pl.BlockSpec(memory_space=pltpu.VMEM), pl.BlockSpec(memory_space=pltpu.VMEM)),
        scratch_shapes=[pltpu.VMEM((KSTEP, size, size), jnp.float32)] * 3,
        compiler_params=pltpu.CompilerParams(vmem_limit_bytes=40 * 1024 * 1024),
        cost_estimate=pl.CostEstimate(flops=40_000_000_000, bytes_accessed=8_000_000, transcendentals=0),
        name="factor",
    )(blocks)


def shards(front, lower_desc, upper_desc, pattern, pivot):
    rows_dev, cols_dev = front.shape
    row_blocks, size = pivot.shape
    grid_rows = lax.axis_size("prow")
    grid_cols = lax.axis_size("pcol")
    own_row = lax.axis_index("prow")
    own_col = lax.axis_index("pcol")
    col_blocks = cols_dev // size
    top_rows = -(-KSTEP // grid_rows) * size
    top_cols = -(-KSTEP // grid_cols) * size
    flags = pattern[0].astype(jnp.bfloat16)
    row_flags = lax.dynamic_slice_in_dim(flags, own_row * row_blocks, row_blocks)
    col_flags = lax.dynamic_slice_in_dim(flags, row_blocks * grid_rows + own_col * col_blocks, col_blocks)
    onehot = (pivot[:, :, None] == jnp.arange(size, dtype=jnp.int32)).astype(jnp.bfloat16)

    def permute(values, weights, kind):
        blocked = values.reshape(row_blocks, size, values.shape[1])
        return jnp.einsum("bij,bjn->bin", weights, blocked, preferred_element_type=kind).reshape(values.shape)

    lower = permute(lower_desc, onehot * row_flags[:, None, None], jnp.bfloat16)
    upper = upper_desc * jnp.repeat(col_flags, size)[None, :]
    initial = permute(front, onehot, jnp.float32)

    def partial(rows, cols):
        return jnp.dot(lower[rows], upper[:, cols], preferred_element_type=jnp.float32)

    def assembled(rows, cols):
        return initial[rows, cols] - lax.psum(partial(rows, cols), "layer")

    left, right = slice(0, top_cols), slice(top_cols, None)
    top, below = slice(0, top_rows), slice(top_rows, None)
    own_left = assembled(slice(0, None), left)
    own_top = jnp.concatenate([own_left[top], assembled(top, right)], axis=1)
    def gather(value, axis):
        count = lax.axis_size(axis)
        own = lax.axis_index(axis)
        held = [value] + [
            lax.ppermute(value, axis, [(i, (i + shift) % count) for i in range(count)])
            for shift in range(1, count)
        ]
        stacked = jnp.stack(held)
        return [
            lax.dynamic_index_in_dim(stacked, lax.rem(own - i + count, count), 0, keepdims=False)
            for i in range(count)
        ]

    rest_part, own_top, own_left = lax.optimization_barrier((partial(below, right), own_top, own_left))
    rest = initial[below, right] - lax.psum(rest_part, "layer")
    halves = gather(own_left[top], "prow")
    wide = gather(jnp.stack(halves), "pcol")
    corner = [[wide[c][r] for c in range(grid_cols)] for r in range(grid_rows)]

    def block(array, r, c):
        return array[r * size : (r + 1) * size, c * size : (c + 1) * size]

    leading = jnp.stack([
        jnp.stack([
            block(corner[i % grid_rows][j % grid_cols], i // grid_rows, j // grid_cols)
            for j in range(KSTEP)
        ])
        for i in range(KSTEP)
    ])
    leading, low_part, top_part = lax.optimization_barrier((leading, own_left[below], own_top))
    columns = gather(low_part, "pcol")
    tops = gather(top_part, "prow")
    packed, inverses = factor(leading)

    upper_rows = []
    for k in range(KSTEP):
        start = k // grid_rows * size
        value = tops[k % grid_rows][start : start + size]
        for j in range(k):
            value = value - jnp.dot(packed[k, j], upper_rows[j], precision=HIGH)
        upper_rows.append(value)
    lower_cols = []
    for k in range(KSTEP):
        start = k // grid_cols * size
        value = columns[k % grid_cols][:, start : start + size]
        for j in range(k):
            value = value - jnp.dot(lower_cols[j], packed[j, k], precision=HIGH)
        lower_cols.append(jnp.dot(value, inverses[k], precision=FINE))
    upper_all = jnp.concatenate(upper_rows, axis=0)
    lower_all = jnp.concatenate(lower_cols, axis=1)

    def trailing(values, multipliers, cols):
        return values - jnp.dot(multipliers, upper_all[:, cols], precision=HIGH)

    def pick(choices, index):
        return lax.dynamic_index_in_dim(choices, index, 0, keepdims=False)

    own_below = jnp.concatenate(
        [
            jnp.where(
                t * grid_cols + own_col < KSTEP,
                pick(jnp.stack(lower_cols), jnp.minimum(t * grid_cols + own_col, KSTEP - 1)),
                trailing(own_left[below, t * size : (t + 1) * size], lower_all, slice(t * size, (t + 1) * size)),
            )
            if grid_cols * (t + 1) > KSTEP
            else pick(jnp.stack(lower_cols), t * grid_cols + own_col)
            for t in range(top_cols // size)
        ]
        + [trailing(rest, lower_all, right)],
        axis=1,
    )
    tops_out = []
    row_stack = jnp.stack(upper_rows)
    for t in range(top_rows // size):
        logical = t * grid_rows + own_row
        if grid_rows * (t + 1) <= KSTEP:
            index = logical
        else:
            index = jnp.minimum(logical, KSTEP - 1)
        value = pick(row_stack, index)
        factors = pick(packed, index)
        pieces = []
        for c in range(top_cols // size):
            column = c * grid_cols + own_col
            inner = pick(factors, jnp.minimum(column, KSTEP - 1))
            pieces.append(jnp.where(column < KSTEP, inner, value[:, c * size : (c + 1) * size]))
        value = jnp.concatenate(pieces + [value[:, top_cols:]], axis=1)
        if grid_rows * (t + 1) > KSTEP:
            source = own_top[t * size : (t + 1) * size]
            lows = []
            own_columns = lax.all_gather(source[:, :top_cols], "pcol")
            for k in range(KSTEP):
                start = k // grid_cols * size
                part = own_columns[k % grid_cols][:, start : start + size]
                for j in range(k):
                    part = part - jnp.dot(lows[j], packed[j, k], precision=HIGH)
                lows.append(jnp.dot(part, inverses[k], precision=FINE))
            full = source - jnp.dot(jnp.concatenate(lows, axis=1), upper_all, precision=HIGH)
            pieces = []
            for c in range(top_cols // size):
                column = c * grid_cols + own_col
                inner = pick(jnp.stack(lows), jnp.minimum(column, KSTEP - 1))
                pieces.append(jnp.where(column < KSTEP, inner, full[:, c * size : (c + 1) * size]))
            full = jnp.concatenate(pieces + [full[:, top_cols:]], axis=1)
            value = jnp.where(logical < KSTEP, value, full)
        tops_out.append(value)
    return jnp.concatenate(tops_out + [own_below], axis=0)


def solution(mesh):
    return jax.shard_map(
        shards,
        mesh=mesh,
        in_specs=(
            P("prow", "pcol"),
            P("prow", "layer"),
            P("layer", "pcol"),
            P("layer", None),
            P("prow", None),
        ),
        out_specs=P("prow", "pcol"),
        check_vma=False,
    )
```

```python
import functools

import jax
import jax.numpy as jnp
from jax import lax
from jax.experimental import pallas as pl
from jax.experimental.pallas import tpu as pltpu
from jax.sharding import PartitionSpec as P

KSTEP = 4
FINE = lax.Precision.HIGHEST
HIGH = lax.Precision.HIGH


def coarse_dot(a, b):
    return jnp.dot(a.astype(jnp.bfloat16), b.astype(jnp.bfloat16), preferred_element_type=jnp.float32)


def fine_dot(a, b):
    return jnp.dot(a, b, precision=FINE, preferred_element_type=jnp.float32)


def gram_bound(scaled):
    low = scaled.astype(jnp.bfloat16)
    gram = lax.dot_general(low, low, (((1,), (1,)), ((), ())), preferred_element_type=jnp.float32)
    return 0.98 / jnp.max(jnp.sum(jnp.abs(gram), axis=1, keepdims=True))


def factor_kernel(a_ref, f_ref, inv_ref, x_ref, r_ref, s_ref):
    size = a_ref.shape[2]
    row = lax.broadcasted_iota(jnp.int32, (size, size), 0)
    col = lax.broadcasted_iota(jnp.int32, (size, size), 1)
    eye = jnp.where(row == col, 1.0, 0.0).astype(jnp.float32)
    f_ref[...] = a_ref[...]

    for b in range(KSTEP):
        block = a_ref[b, b]
        peak = jnp.max(jnp.abs(block), axis=1, keepdims=True)
        scale = jnp.where(peak > 0.0, 1.0 / jnp.where(peak > 0.0, peak, 1.0), 1.0)
        s_ref[b] = jnp.broadcast_to(scale, (size, size))
        scaled = block * scale
        start = scaled.T * gram_bound(scaled)
        x_ref[b] = start
        r_ref[b] = eye - coarse_dot(scaled, start)

    def worst():
        return functools.reduce(jnp.maximum, [jnp.sum(r_ref[b] * r_ref[b]) for b in range(KSTEP)])

    def coarse(state):
        for b in range(KSTEP):
            left = r_ref[b]
            start = x_ref[b]
            once = start + coarse_dot(start, left)
            twice = once + coarse_dot(once, coarse_dot(left, left))
            x_ref[b] = twice
            r_ref[b] = eye - coarse_dot(a_ref[b, b] * s_ref[b], twice)
        return state[0] + 1, worst()

    lax.while_loop(lambda s: (s[1] > 0.1) & (s[0] < 12), coarse, (jnp.int32(0), worst()))

    for k in range(KSTEP):
        scale = s_ref[k]
        scaled = f_ref[k, k] * scale
        r_ref[k] = eye - fine_dot(scaled, x_ref[k])
        near = jnp.sum(r_ref[k] * r_ref[k])

        @pl.when(jnp.logical_not(near < 0.5))
        def restart():
            start = scaled.T * gram_bound(scaled)
            x_ref[k] = start
            r_ref[k] = eye - fine_dot(scaled, start)

        def fine(state):
            x_ref[k] = x_ref[k] + fine_dot(x_ref[k], r_ref[k])
            left = eye - fine_dot(f_ref[k, k] * s_ref[k], x_ref[k])
            r_ref[k] = left
            return state[0] + 1, jnp.sum(left * left)

        lax.while_loop(
            lambda s: (s[1] > 1e-6) & (s[0] < 60), fine, (jnp.int32(0), jnp.sum(r_ref[k] * r_ref[k]))
        )
        across = jnp.sum(eye * scale, axis=0, keepdims=True)
        inverse = (x_ref[k] + fine_dot(x_ref[k], r_ref[k])) * across
        inv_ref[k] = inverse
        for i in range(k + 1, KSTEP):
            f_ref[i, k] = fine_dot(f_ref[i, k], inverse)
            for j in range(k + 1, KSTEP):
                f_ref[i, j] = f_ref[i, j] - fine_dot(f_ref[i, k], f_ref[k, j])


def factor(blocks):
    size = blocks.shape[2]
    return pl.pallas_call(
        factor_kernel,
        out_shape=(
            jax.ShapeDtypeStruct(blocks.shape, jnp.float32),
            jax.ShapeDtypeStruct((KSTEP, size, size), jnp.float32),
        ),
        in_specs=[pl.BlockSpec(memory_space=pltpu.VMEM)],
        out_specs=(pl.BlockSpec(memory_space=pltpu.VMEM), pl.BlockSpec(memory_space=pltpu.VMEM)),
        scratch_shapes=[pltpu.VMEM((KSTEP, size, size), jnp.float32)] * 3,
        compiler_params=pltpu.CompilerParams(vmem_limit_bytes=40 * 1024 * 1024),
        cost_estimate=pl.CostEstimate(flops=40_000_000_000, bytes_accessed=8_000_000, transcendentals=0),
        name="factor",
    )(blocks)


def shards(front, lower_desc, upper_desc, pattern, pivot):
    rows_dev, cols_dev = front.shape
    row_blocks, size = pivot.shape
    grid_rows = lax.axis_size("prow")
    grid_cols = lax.axis_size("pcol")
    own_row = lax.axis_index("prow")
    own_col = lax.axis_index("pcol")
    col_blocks = cols_dev // size
    top_rows = -(-KSTEP // grid_rows) * size
    top_cols = -(-KSTEP // grid_cols) * size
    flags = pattern[0].astype(jnp.bfloat16)
    row_flags = lax.dynamic_slice_in_dim(flags, own_row * row_blocks, row_blocks)
    col_flags = lax.dynamic_slice_in_dim(flags, row_blocks * grid_rows + own_col * col_blocks, col_blocks)
    onehot = (pivot[:, :, None] == jnp.arange(size, dtype=jnp.int32)).astype(jnp.bfloat16)

    def permute(values, weights, kind):
        blocked = values.reshape(row_blocks, size, values.shape[1])
        return jnp.einsum("bij,bjn->bin", weights, blocked, preferred_element_type=kind).reshape(values.shape)

    lower = permute(lower_desc, onehot * row_flags[:, None, None], jnp.bfloat16)
    upper = upper_desc * jnp.repeat(col_flags, size)[None, :]
    initial = permute(front, onehot, jnp.float32)

    def partial(rows, cols):
        return jnp.dot(lower[rows], upper[:, cols], preferred_element_type=jnp.float32)

    def assembled(rows, cols):
        return initial[rows, cols] - lax.psum(partial(rows, cols), "layer")

    left, right = slice(0, top_cols), slice(top_cols, None)
    top, below = slice(0, top_rows), slice(top_rows, None)
    own_left = assembled(slice(0, None), left)
    own_top = jnp.concatenate([own_left[top], assembled(top, right)], axis=1)
    def gather(value, axis):
        count = lax.axis_size(axis)
        own = lax.axis_index(axis)
        held = [value] + [
            lax.ppermute(value, axis, [(i, (i + shift) % count) for i in range(count)])
            for shift in range(1, count)
        ]
        stacked = jnp.stack(held)
        return [
            lax.dynamic_index_in_dim(stacked, lax.rem(own - i + count, count), 0, keepdims=False)
            for i in range(count)
        ]

    def exchanged_sum(total):
        count = lax.axis_size("layer")
        own = lax.axis_index("layer")
        bits = [1 << n for n in range(count.bit_length() - 1)]
        if 1 << len(bits) != count or total.shape[0] % count:
            return lax.psum(total, "layer")

        def swap(value, bit):
            return lax.ppermute(value, "layer", [(i, i ^ bit) for i in range(count)])

        for bit in bits:
            half = total.shape[0] // 2
            high = lax.rem(own // bit, 2) == 1
            low_half, high_half = total[:half], total[half:]
            received = swap(jnp.where(high, low_half, high_half), bit)
            total = jnp.where(high, high_half, low_half) + received
        for bit in reversed(bits):
            high = lax.rem(own // bit, 2) == 1
            received = swap(total, bit)
            total = jnp.concatenate([jnp.where(high, received, total), jnp.where(high, total, received)], axis=0)
        return total

    rest = initial[below, right] - exchanged_sum(partial(below, right))
    halves = gather(own_left[top], "prow")
    wide = gather(jnp.stack(halves), "pcol")
    corner = [[wide[c][r] for c in range(grid_cols)] for r in range(grid_rows)]

    def block(array, r, c):
        return array[r * size : (r + 1) * size, c * size : (c + 1) * size]

    leading = jnp.stack([
        jnp.stack([
            block(corner[i % grid_rows][j % grid_cols], i // grid_rows, j // grid_cols)
            for j in range(KSTEP)
        ])
        for i in range(KSTEP)
    ])
    leading, low_part, top_part = lax.optimization_barrier((leading, own_left[below], own_top))
    columns = gather(low_part, "pcol")
    tops = gather(top_part, "prow")
    packed, inverses = factor(leading)

    upper_rows = []
    for k in range(KSTEP):
        start = k // grid_rows * size
        value = tops[k % grid_rows][start : start + size]
        for j in range(k):
            value = value - jnp.dot(packed[k, j], upper_rows[j], precision=HIGH)
        upper_rows.append(value)
    lower_cols = []
    for k in range(KSTEP):
        start = k // grid_cols * size
        value = columns[k % grid_cols][:, start : start + size]
        for j in range(k):
            value = value - jnp.dot(lower_cols[j], packed[j, k], precision=HIGH)
        lower_cols.append(jnp.dot(value, inverses[k], precision=FINE))
    upper_all = jnp.concatenate(upper_rows, axis=0)
    lower_all = jnp.concatenate(lower_cols, axis=1)

    def trailing(values, multipliers, cols):
        return values - jnp.dot(multipliers, upper_all[:, cols], precision=HIGH)

    def pick(choices, index):
        return lax.dynamic_index_in_dim(choices, index, 0, keepdims=False)

    own_below = jnp.concatenate(
        [
            jnp.where(
                t * grid_cols + own_col < KSTEP,
                pick(jnp.stack(lower_cols), jnp.minimum(t * grid_cols + own_col, KSTEP - 1)),
                trailing(own_left[below, t * size : (t + 1) * size], lower_all, slice(t * size, (t + 1) * size)),
            )
            if grid_cols * (t + 1) > KSTEP
            else pick(jnp.stack(lower_cols), t * grid_cols + own_col)
            for t in range(top_cols // size)
        ]
        + [trailing(rest, lower_all, right)],
        axis=1,
    )
    tops_out = []
    row_stack = jnp.stack(upper_rows)
    for t in range(top_rows // size):
        logical = t * grid_rows + own_row
        if grid_rows * (t + 1) <= KSTEP:
            index = logical
        else:
            index = jnp.minimum(logical, KSTEP - 1)
        value = pick(row_stack, index)
        factors = pick(packed, index)
        pieces = []
        for c in range(top_cols // size):
            column = c * grid_cols + own_col
            inner = pick(factors, jnp.minimum(column, KSTEP - 1))
            pieces.append(jnp.where(column < KSTEP, inner, value[:, c * size : (c + 1) * size]))
        value = jnp.concatenate(pieces + [value[:, top_cols:]], axis=1)
        if grid_rows * (t + 1) > KSTEP:
            source = own_top[t * size : (t + 1) * size]
            lows = []
            own_columns = lax.all_gather(source[:, :top_cols], "pcol")
            for k in range(KSTEP):
                start = k // grid_cols * size
                part = own_columns[k % grid_cols][:, start : start + size]
                for j in range(k):
                    part = part - jnp.dot(lows[j], packed[j, k], precision=HIGH)
                lows.append(jnp.dot(part, inverses[k], precision=FINE))
            full = source - jnp.dot(jnp.concatenate(lows, axis=1), upper_all, precision=HIGH)
            pieces = []
            for c in range(top_cols // size):
                column = c * grid_cols + own_col
                inner = pick(jnp.stack(lows), jnp.minimum(column, KSTEP - 1))
                pieces.append(jnp.where(column < KSTEP, inner, full[:, c * size : (c + 1) * size]))
            full = jnp.concatenate(pieces + [full[:, top_cols:]], axis=1)
            value = jnp.where(logical < KSTEP, value, full)
        tops_out.append(value)
    return jnp.concatenate(tops_out + [own_below], axis=0)


def solution(mesh):
    return jax.shard_map(
        shards,
        mesh=mesh,
        in_specs=(
            P("prow", "pcol"),
            P("prow", "layer"),
            P("layer", "pcol"),
            P("layer", None),
            P("prow", None),
        ),
        out_specs=P("prow", "pcol"),
        check_vma=False,
    )
```
